256 devices in a mesh: fsdp: 32 (over x, y, core), dp: 8 (over z).
Axes of the slice: x: 4, y: 4, z: 8, core: 2. Of those that a mesh axis runs over, the one named last changes fastest.
Arguments:
- tokens: bfloat16 [32, 2048, 8192], P('fsdp', 'dp'), may hold values from -6 to 6
- norm_gain: float32 [8192], replicated, may hold values from 0.6 to 35
- old_master: float32 [3072, 2048], P('fsdp'), may hold values from -0.0625 to 0.0625
- route_peer: int32 [32, 96], replicated, may hold values from 0 to 31, as said below
- route_slot: int32 [32, 96], replicated, may hold values from 0 to 95
- out_weight: bfloat16 [512, 8192], P(None, 'fsdp'), may hold values from -1.5 to 1.5
- doc_lengths: int32 [32, 8], P('fsdp'), may hold values from 1 to 1024, 2048 in all within a row
Outputs:
- attn_update: bfloat16 [32, 2048, 8192], P('fsdp', 'dp')
- new_master: float32 [3072, 2048], P('fsdp')
The draws below stay inside these ranges and needn't reach their ends.
Inputs may be any that keep to these rules, and one draw needn't show every extreme that they name: For every old owner i and every new owner j, route_peer[i, p] == j for at most 6 positions p, and for exactly 6 of them with one j per i; every new owner receives exactly 96 blocks, one for each slot, so (route_peer, route_slot) is a bijection onto owner and slot.
All inputs are finite; a program needn't handle non-finite values.
Results may differ from the reference program's by a relative error of at most 0.0095.
The reference program's roundings to bfloat16 on the way (of `w_in`, `normed` and `attended`) count: a program that leaves them out, or rounds other values in their place, can miss the bound.
Values may be sent and summed in bfloat16 or wider, within the bound.
A program may use at most 128 MiB of HBM per device.

```python
import math
import jax
import jax.numpy as jnp
import numpy as np
from jax import lax

D = 8192
HD = 128
HQ = 4
BLK = 2048
NDOCS = 8
QKV = 768
OW = 512
L = 2048
SEQS = 32
R = 96
MOST = 6
N_FSDP = 32


def route_tables(key):
    first, second, third = jax.random.split(key, 3)
    drawn = jax.random.permutation(first, N_FSDP)
    place = jnp.arange(N_FSDP)
    priority = jnp.where(drawn == N_FSDP // 2, -2, jnp.where(drawn == 1, -1, place))
    shift_values = drawn[jnp.argsort(priority)]
    virtual = jnp.arange(R)
    grouping = jnp.where(virtual < MOST, 0, (virtual - MOST) % max(N_FSDP - 1, 1) + 1)
    offsets = shift_values[grouping]
    slot_order = jax.random.permutation(second, R)
    ranking = jax.random.randint(third, (N_FSDP, R), 0, 1 << 20) * R + virtual[None, :]
    ordering = jnp.argsort(ranking, axis=1)
    senders = jnp.arange(N_FSDP)[:, None]
    peers = (senders + offsets[ordering]) % N_FSDP
    slots = slot_order[ordering]
    return (peers.astype(jnp.int32), slots.astype(jnp.int32))


def draw_route_peer(key, part):
    peers, slots = route_tables(key)
    return peers


def draw_route_slot(key, part):
    peers, slots = route_tables(key)
    return slots


def draw_norm_gain(key, part):
    key = jax.random.fold_in(key, 11)
    first = jax.random.fold_in(key, 0)
    base = jax.random.uniform(first, (D,), jnp.float32, 0.6, 1.4)
    return base


def steps_of(key, dims, shards, least, high):
    factor_of, own = 1.0, jax.random.fold_in(key, 6)
    for dim, parts in shards:
        heights = jnp.exp(jax.random.uniform(jax.random.fold_in(own, dim), (parts,), jnp.float32, least / len(shards), high / len(shards)))
        factor_of = factor_of * jnp.repeat(heights, dims[dim] // parts).reshape([-1 if axis == dim else 1 for axis in range(len(dims))])
    return factor_of


def length_profile(count, total, most, skew):
    loads = [(1 << 20) // math.isqrt(standing ** skew) + 1 for standing in range(2, count + 1)]
    rest, holding = total - most - (count - 1), [1] * (count - 1)
    while rest > 0:
        candidates = [i for i in range(count - 1) if holding[i] < most]
        pool, budget = sum([loads[i] for i in candidates]), rest
        for i in candidates:
            addition = min(most - holding[i], max(1, budget * loads[i] // pool), rest)
            holding[i] = holding[i] + addition
            rest = rest - addition
    return np.array([most] + holding)


def uneven(stream_key, count, total, limit, lean):
    if count == 2:
        one = jax.random.randint(stream_key, (), max(1, total - limit), min(limit, total - 1) + 1)
        return jnp.stack([one, total - one])
    sizes = jnp.asarray(length_profile(count, total, limit, lean), jnp.int32)
    twos = (count - 1) // 2
    giver, sink = sizes[1:1 + 2 * twos:2], sizes[2:2 + 2 * twos:2]
    slack = jnp.minimum(giver - 1, limit - sink)
    moved = jax.random.randint(jax.random.fold_in(stream_key, 1), (twos,), 0, 1 << 20) % (slack + 1)
    sizes = sizes.at[1:1 + 2 * twos:2].set(giver - moved).at[2:2 + 2 * twos:2].set(sink + moved)
    return sizes[jax.random.permutation(jax.random.fold_in(stream_key, 2), count)]


def scatter_about(key, shape, width, most, shards=(), kind=jnp.bfloat16):
    gain = steps_of(key, shape, shards, -0.22, 0.18) if shards else 1.0
    values = jax.random.normal(key, shape, jnp.float32) * width * gain
    return jnp.minimum(jnp.maximum(values, -most), most).astype(kind)


def setup_inputs(seed: int = 0) -> dict:
    splits = jax.random.split(jax.random.key(seed), 8)
    return {
        "tokens": scatter_about(splits[0], (SEQS, L, D), 1.0, 6.0, ((0, 32), (1, 8))),
        "norm_gain": draw_norm_gain(jax.random.fold_in(splits[7], 71), 0),
        "old_master": scatter_about(splits[2], (N_FSDP * R, BLK), D ** -0.5, 0.0625, ((0, 32),), jnp.float32),
        "route_peer": draw_route_peer(jax.random.fold_in(splits[7], 71), 0),
        "route_slot": draw_route_slot(jax.random.fold_in(splits[7], 71), 0),
        "out_weight": scatter_about(splits[5], (OW, D), (HD // 8) ** -0.5, 1.5, ((1, 32),)),
        "doc_lengths": jax.vmap(lambda own: uneven(own, NDOCS, L, L // 2, 2))(jax.random.split(splits[6], SEQS)).reshape((SEQS, NDOCS)).astype(jnp.int32),
    }


theta_base = 500000.0
epsilon = 1e-05
masked_score = -1e+30

def rope_tables(positions):
    half_size = HD // 2
    inverse = jnp.exp(-jnp.log(jnp.float32(theta_base)) * jnp.arange(half_size, dtype=jnp.float32) * 2.0 / HD)
    angles = positions.astype(jnp.float32)[:, None] * inverse[None, :]
    return (jnp.cos(angles), jnp.sin(angles))

def rotate(values, cosine, sine):
    half_size = HD // 2
    first = values[..., :half_size]
    second = values[..., half_size:]
    return jnp.concatenate([first * cosine - second * sine, second * cosine + first * sine], axis=-1)

def reference(tokens, norm_gain, old_master, route_peer, route_slot, out_weight, doc_lengths):
    destination = (route_peer * R + route_slot).reshape(-1)
    new_master = jnp.zeros_like(old_master).at[destination].set(old_master)
    w_in = new_master.astype(jnp.bfloat16).reshape(D, QKV)
    positions = jnp.arange(L, dtype=jnp.int32)
    cosine, sine = rope_tables(positions)
    scale = 1.0 / jnp.sqrt(jnp.float32(HD))

    def one_sequence(inputs):
        sequence, lengths = inputs
        values_f = sequence.astype(jnp.float32)
        square_mean = lax.optimization_barrier(jnp.mean(values_f * values_f, axis=-1, keepdims=True))
        normed = (values_f * lax.rsqrt(square_mean + epsilon) * norm_gain).astype(jnp.bfloat16)
        projection = jnp.dot(normed, w_in, preferred_element_type=jnp.float32)
        queries = projection[:, :OW].reshape(L, HQ, HD)
        queries = rotate(queries, cosine[:, None, :], sine[:, None, :]).astype(jnp.bfloat16)
        keys = rotate(projection[:, OW:OW + HD], cosine, sine).astype(jnp.bfloat16)
        values = projection[:, OW + HD:].astype(jnp.bfloat16)
        doc_ends = jnp.cumsum(lengths).astype(jnp.int32)
        doc_index = lax.optimization_barrier(jnp.sum((positions[:, None] >= doc_ends[None, :]).astype(jnp.int32), axis=1))
        visible = (positions[None, :] <= positions[:, None]) & (doc_index[None, :] == doc_index[:, None])
        scores = jnp.einsum('qhd,kd->hqk', queries.astype(jnp.float32), keys.astype(jnp.float32)) * scale
        scores = jnp.where(visible[None, :, :], scores, masked_score)
        maximum = lax.optimization_barrier(jnp.max(scores, axis=-1, keepdims=True))
        expterm = jnp.where(visible[None, :, :], jnp.exp(scores - maximum), 0.0)
        totals = lax.optimization_barrier(jnp.sum(expterm, axis=-1))
        weights = expterm.astype(jnp.bfloat16)
        attended = jnp.einsum('hqk,kd->hqd', weights.astype(jnp.float32), values.astype(jnp.float32))
        attended = attended / totals[:, :, None]
        attended = jnp.transpose(attended, (1, 0, 2)).reshape(L, OW).astype(jnp.bfloat16)
        return jnp.dot(attended, out_weight, preferred_element_type=jnp.float32).astype(jnp.bfloat16)
    attn_update = lax.map(one_sequence, (tokens, doc_lengths))
    return (attn_update, new_master)
```

```python
import jax
import jax.numpy as jnp
import numpy as np
from jax import lax
from jax.experimental import pallas as pl
from jax.experimental.pallas import tpu as pltpu
from jax.sharding import PartitionSpec as P

HD = 128
HQ = 4
BLK = 2048
theta_base = 500000.0
epsilon = 1e-05
masked_score = -1e30
MESH = pl.DeviceIdType.MESH
F32, BF16, I32 = jnp.float32, jnp.bfloat16, jnp.int32

NF, NZ = 32, 8
ROWS, D = 256, 8192
QW, KVW, W = 512, 256, 768
LANES = 128
COLS = ((QW, KVW), (0, QW))
BACK = 4


def dot(a, b):
    return jnp.dot(a, b, preferred_element_type=F32)


def iota(shape, axis):
    return lax.broadcasted_iota(I32, shape, axis)


def hot(condition):
    return jnp.where(condition, 1.0, 0.0).astype(BF16)


def kernel(
    tok_hbm, gain, old, peer, slot, ow_hbm, docs, cos_r, sin_r, cos_z, sin_z,
    out_hbm, nm_hbm,
    tok, oldb, sendbuf, inbuf, wbuf, obuf, kvbuf, acc, att, staged, nm, bias,
    local_sem, a2a_s, a2a_r, w_s, w_r, sib_s, sib_r, ow_s, ow_r, oz_s, oz_r, os_s, os_r, kv_s, kv_r, out_sem,
):
    me = lax.axis_index("fsdp")
    z = lax.axis_index("dp")
    c = lax.rem(me, 2)
    y = lax.rem(lax.div(me, 2), 4)
    x = lax.div(me, 8)
    place = x * 4 + y
    sibling = me + 1 - 2 * c
    up, down = lax.rem(z + 1, NZ), lax.rem(z + NZ - 1, NZ)

    def panel(dx, dy, core):
        return lax.rem(x + 4 - dx, 4) * 8 + lax.rem(y + 4 - dy, 4) * 2 + core

    def remote(src, dst, send, recv, **to):
        return pltpu.make_async_remote_copy(
            src_ref=src, dst_ref=dst, send_sem=send, recv_sem=recv, device_id=to, device_id_type=MESH
        )

    barrier = pltpu.get_barrier_semaphore()

    @pl.loop(1, NF)
    def _(k):
        pl.semaphore_signal(barrier, inc=1, device_id={"fsdp": lax.rem(me + k, NF)}, device_id_type=MESH)

    for to in (up, down):
        pl.semaphore_signal(barrier, inc=1, device_id={"dp": to}, device_id_type=MESH)

    tokens_in = pltpu.make_async_copy(tok_hbm, tok, local_sem.at[0])
    tokens_in.start()
    own_rows = pl.ds(pl.multiple_of(z * 64, 64), 64)
    own_out = pltpu.make_async_copy(ow_hbm.at[own_rows, :], obuf.at[c, place, own_rows, :], local_sem.at[1])
    own_out.start()

    for part in range(8):
        oldb[pl.ds(part * LANES, 96), :] = old[:, pl.ds(part * 256, 256)].astype(BF16)
        oldb[pl.ds(part * LANES + 96, 32), :] = jnp.zeros((32, 256), BF16)
    before = hot(iota((LANES, LANES), 0) < iota((LANES, LANES), 1))
    own_peer = peer[pl.ds(me, 1), :]
    mine = iota((NF, LANES), 0) == own_peer
    rank = jnp.sum(jnp.where(mine, dot(hot(mine), before), 0.0), axis=0, keepdims=True).astype(I32)
    base = jnp.where(own_peer >= 0, own_peer * 16 + (rank & 1) * 8, -1000)
    for g in range(3):
        target = jnp.where((rank >> 1) == g, base, -1000)
        rows = iota((NF * 16, LANES), 0)
        select = jnp.concatenate([hot(rows == target + part) for part in range(8)], axis=1)
        sendbuf[:, pl.ds(g * 256, 256)] = dot(select, oldb[...]).astype(BF16)

    pl.semaphore_wait(barrier, NF - 1 + 2)

    def sixteen(f):
        return pl.ds(pl.multiple_of(f * 16, 16), 16)

    def a2a(to):
        return remote(
            sendbuf.at[sixteen(to), :], inbuf.at[sixteen(me), :], a2a_s.at[to], a2a_r.at[me], fsdp=to
        )

    def a2a_from(f):
        return remote(
            sendbuf.at[sixteen(f), :], inbuf.at[sixteen(f), :], a2a_s.at[f], a2a_r.at[f], fsdp=f
        )

    @pl.loop(1, NF)
    def _(k):
        a2a(lax.rem(me + k, NF)).start()

    inbuf[sixteen(me), :] = sendbuf[sixteen(me), :]

    def ow_to(k):
        to = lax.rem(place + k, 16)
        return remote(
            ow_hbm.at[own_rows, :], obuf.at[c, place, own_rows, :], ow_s.at[to], ow_r.at[place], fsdp=to * 2 + c
        )

    def ow_from(f):
        return remote(
            ow_hbm.at[own_rows, :], obuf.at[c, f, own_rows, :], ow_s.at[f], ow_r.at[f], fsdp=f * 2 + c
        )

    @pl.loop(1, 16)
    def _(k):
        ow_to(k).start()

    tokens_in.wait()

    @pl.loop(0, ROWS // 16)
    def _(i):
        rows = pl.ds(pl.multiple_of(i * 16, 16), 16)
        values = tok[rows, :].astype(F32)
        square_mean = jnp.mean(values * values, axis=-1, keepdims=True)
        tok[rows, :] = (values * lax.rsqrt(square_mean + epsilon) * gain[...]).astype(BF16)

    ours = peer[...] == me
    arrival = dot(hot(ours), before)
    lane = iota((1, NF * 16), 1)
    holder = iota((NF, NF * 16), 0) == (iota((NF, NF * 16), 1) >> 4)
    odd = ((iota((NF, NF * 16), 1) >> 3) & 1) == 1
    slots = []
    for r in range(6):
        found = ours & (arrival == float(r))
        slots.append(jnp.sum(jnp.where(found, slot[...] + 1, 0), axis=1, keepdims=True) - 1)
    slot_rows = []
    for g in range(3):
        spread = jnp.where(odd, slots[2 * g + 1], slots[2 * g])
        slot_rows.append(jnp.sum(jnp.where(holder, spread, 0), axis=0, keepdims=True))

    @pl.loop(1, NF)
    def _(k):
        a2a_from(lax.rem(me + NF - k, NF)).wait_recv()

    def panel_rows(f):
        return pl.ds(pl.multiple_of(f * ROWS, ROWS), ROWS)

    for g in range(3):
        total = jnp.zeros((256, 256), F32)
        for h in range(3):
            flat = slot_rows[h] * 8 + (lane & 7)
            row = (flat * 21846) >> 16
            row = jnp.where((slot_rows[h] >= 0) & (flat - row * 3 == g), row, -1)
            total += dot(hot(iota((256, NF * 16), 0) == row), inbuf[:, pl.ds(h * 256, 256)])
        wbuf[panel_rows(me), pl.ds(g * 256, 256)] = total.astype(BF16)

    def coords(half, first, second):
        return (first, second) if half == 0 else (second, first)

    def neighbour(axis, step):
        if axis == 0:
            return lax.rem(x + 4 + step, 4) * 8 + y * 2 + c
        return x * 8 + lax.rem(y + 4 + step, 4) * 2 + c

    def ring(stage, half, phase, kind, sending):
        step = 1 if kind in (0, 2) else -1
        arrives = {0: 1, 1: 3, 2: 2, 3: 2}[kind]
        leaves = {0: 0, 1: 0, 2: 1, 3: 3}[kind]
        along = leaves if sending else arrives
        if phase == 0:
            dx, dy = coords(half, along, 0)
            axis = half
        else:
            dx, dy = coords(half, phase - 1, along)
            axis = 1 - half
        start = panel(dx, dy, c) * ROWS + half * 128 + (64 if kind == 3 else 0)
        size = 64 if kind >= 2 else 128
        first, width = COLS[stage]
        ref = wbuf.at[pl.ds(pl.multiple_of(start, 64), size), pl.ds(first, width)]
        index = ((stage * 2 + half) * 5 + phase) * 4 + kind
        return remote(ref, ref, w_s.at[index], w_r.at[index], fsdp=neighbour(axis, step))

    def go(stage, phase, kinds):
        for kind in kinds:
            for half in range(2):
                ring(stage, half, phase, kind, True).start()

    def come(stage, phase, kinds):
        for kind in kinds:
            for half in range(2):
                ring(stage, half, phase, kind, False).wait_recv()

    def side(stage, dx, dy, core):
        first, width = COLS[stage]
        ref = wbuf.at[panel_rows(panel(dx, dy, core)), pl.ds(first, width)]
        index = stage * 16 + dx * 4 + dy
        return remote(ref, ref, sib_s.at[index], sib_r.at[index], fsdp=sibling)

    def share(stage, places):
        for dx, dy in places:
            side(stage, dx, dy, c).start()

    def multiply(stage, places, other):
        first, width = COLS[stage]
        for dx, dy in places:
            if other:
                side(stage, dx, dy, 1 - c).wait_recv()
            f = panel(dx, dy, 1 - c if other else c)
            columns = pl.ds(first, width)
            acc[:, columns] += dot(tok[:, panel_rows(f)], wbuf[panel_rows(f), columns])

    near = [(0, 0)]
    cross = [(1, 0), (3, 0), (0, 1), (0, 3)]
    corner = [(1, 1), (1, 3), (3, 1), (3, 3)]
    two = [(2, 0), (0, 2)]
    knight = [(1, 2), (3, 2), (2, 1), (2, 3)]
    far = [(2, 2)]

    def open_stage(stage):
        go(stage, 0, (0, 1))
        go(stage, 1, (0, 1))
        share(stage, near)

    def step_one(stage):
        come(stage, 0, (0,))
        go(stage, 0, (2,))
        go(stage, 2, (0, 1))
        come(stage, 0, (1,))
        go(stage, 0, (3,))
        go(stage, 4, (0, 1))

    def step_two(stage):
        come(stage, 1, (0,))
        go(stage, 1, (2,))
        come(stage, 1, (1,))
        go(stage, 1, (3,))
        share(stage, cross)

    def step_three(stage):
        come(stage, 0, (2, 3))
        go(stage, 3, (0, 1))

    def step_four(stage):
        for phase in (2, 4):
            come(stage, phase, (0,))
            go(stage, phase, (2,))
            come(stage, phase, (1,))
            go(stage, phase, (3,))
        share(stage, corner)

    def step_five(stage):
        come(stage, 1, (2, 3))
        share(stage, two)
        come(stage, 3, (0,))
        go(stage, 3, (2,))
        come(stage, 3, (1,))
        go(stage, 3, (3,))

    def step_six(stage):
        come(stage, 2, (2, 3))
        come(stage, 4, (2, 3))
        share(stage, knight)

    def step_seven(stage):
        come(stage, 3, (2, 3))
        share(stage, far)

    def oz(way, step, sending):
        at = z - (step - 1 if sending else step) if way == 0 else z + (step - 1 if sending else step)
        rows = pl.ds(pl.multiple_of(lax.rem(at + NZ, NZ) * 64, 64), 64)
        ref = obuf.at[c, :, rows, :]
        index = way * 4 + step - 1
        return remote(ref, ref, oz_s.at[index], oz_r.at[index], dp=up if way == 0 else down)

    def o_side(back, core):
        rows = pl.ds(pl.multiple_of(lax.rem(z + NZ - back, NZ) * 64, 64), 64)
        ref = obuf.at[core, :, rows, :]
        return remote(ref, ref, os_s.at[back], os_r.at[back], fsdp=sibling)

    def oz_next(step):
        if step <= 3:
            oz(0, step, False).wait_recv()
            if step < 3:
                oz(0, step + 1, True).start()
            o_side(step, c).start()
        oz(1, step, False).wait_recv()
        if step < 4:
            oz(1, step + 1, True).start()
        o_side(NZ - step, c).start()

    def kv(step, sending):
        src = kvbuf.at[pl.ds((step - 1) * ROWS, ROWS), :]
        dst = kvbuf.at[pl.ds(step * ROWS, ROWS), :]
        return remote(src, dst, kv_s.at[step - 1], kv_r.at[step - 1], dp=up)

    open_stage(0)

    @pl.loop(1, 16)
    def _(k):
        ow_from(lax.rem(place + 16 - k, 16)).wait_recv()

    own_out.wait()
    oz(0, 1, True).start()
    oz(1, 1, True).start()
    o_side(0, c).start()

    step_one(0)
    acc[...] = jnp.zeros_like(acc)
    for part in range(8):
        total = jnp.zeros((96, 256), F32)
        for h in range(3):
            row = jnp.where((lane & 7) == part, slot_rows[h], -1)
            total += dot(hot(iota((96, NF * 16), 0) == row), inbuf[:, pl.ds(h * 256, 256)])
        nm[:, pl.ds(part * 256, 256)] = total
    nm_out = pltpu.make_async_copy(nm, nm_hbm, local_sem.at[2])
    nm_out.start()
    step_two(0)
    multiply(0, near, False)
    step_three(0)
    multiply(0, near, True)
    open_stage(1)
    step_four(0)
    multiply(0, cross, False)
    step_five(0)
    multiply(0, cross, True)
    multiply(0, corner, False)
    step_one(1)
    step_six(0)
    oz_next(1)
    multiply(0, corner + two, True)
    multiply(0, two, False)
    step_two(1)
    step_seven(0)
    multiply(0, knight + far, False)
    step_three(1)
    multiply(0, knight + far, True)

    cz, sz = cos_z[pl.ds(z, 1), :], sin_z[pl.ds(z, 1), :]
    cosine = cos_r[...] * cz - sin_r[...] * sz
    sine = sin_r[...] * cz + cos_r[...] * sz
    sine = jnp.where(iota((ROWS, HD), 1) < HD // 2, -sine, sine)

    def rotate(values):
        return (values * cosine + pltpu.roll(values, HD // 2, 1) * sine).astype(BF16)

    kvbuf[pl.ds(0, ROWS), pl.ds(0, HD)] = rotate(acc[:, pl.ds(QW, HD)])
    kvbuf[pl.ds(0, ROWS), pl.ds(HD, HD)] = acc[:, pl.ds(QW + HD, HD)].astype(BF16)
    kv(1, True).start()
    step_four(1)
    multiply(1, near + cross, False)
    kv(1, False).wait_recv()
    kv(2, True).start()
    step_five(1)
    oz_next(2)
    multiply(1, near + cross, True)
    kv(2, False).wait_recv()
    kv(3, True).start()
    multiply(1, corner + two, False)
    step_six(1)
    multiply(1, corner + two, True)
    kv(3, False).wait_recv()
    kv(4, True).start()

    query = z * ROWS + iota((ROWS, 1), 0)
    begin = jnp.zeros((ROWS, 1), I32)
    end = jnp.int32(0)
    for d in range(8):
        end = end + docs[0, d]
        begin = jnp.where(query >= end, end, begin)
    for back in range(BACK + 1):
        key = (z - back) * ROWS + iota((ROWS, ROWS), 1)
        bias[:, pl.ds(back * ROWS, ROWS)] = jnp.where((key <= query) & (key >= begin), 0.0, masked_score)

    step_seven(1)
    oz_next(3)
    multiply(1, knight + far, False)
    multiply(1, knight + far, True)
    kv(4, False).wait_recv()

    scale = 1.0 / np.sqrt(np.float32(HD))
    for h in range(HQ):
        columns = pl.ds(h * HD, HD)
        queries = rotate(acc[:, columns])
        scores = lax.dot_general(
            queries, kvbuf[:, pl.ds(0, HD)], (((1,), (1,)), ((), ())), preferred_element_type=F32
        )
        scores = scores * scale + bias[...]
        expterm = jnp.exp(scores - jnp.max(scores, axis=1, keepdims=True))
        denom = jnp.sum(expterm, axis=1, keepdims=True)
        att[:, columns] = (dot(expterm.astype(BF16), kvbuf[:, pl.ds(HD, HD)]) / denom).astype(BF16)

    oz_next(4)
    for back in range(NZ):
        o_side(back, 1 - c).wait_recv()

    def out_copy(part):
        columns = pl.ds(part * 2048, 2048)
        return pltpu.make_async_copy(staged.at[:, columns], out_hbm.at[:, columns], out_sem.at[part])

    for part in range(4):
        for i in range(8):
            f = part * 8 + i
            staged[:, pl.ds(f * 256, 256)] = dot(att[...], obuf[f % 2, f // 2]).astype(BF16)
        out_copy(part).start()

    @pl.loop(1, NF)
    def _(k):
        a2a(lax.rem(me + k, NF)).wait_send()

    @pl.loop(1, 16)
    def _(k):
        ow_to(k).wait_send()

    for stage in range(2):
        for phase in range(5):
            for kind in range(4):
                for half in range(2):
                    ring(stage, half, phase, kind, True).wait_send()
        for dx in range(4):
            for dy in range(4):
                side(stage, dx, dy, c).wait_send()
    for step in range(1, 5):
        if step < 4:
            oz(0, step, True).wait_send()
        oz(1, step, True).wait_send()
        kv(step, True).wait_send()
    for back in range(NZ):
        o_side(back, c).wait_send()
    nm_out.wait()
    for part in range(4):
        out_copy(part).wait()


def rotation_tables():
    inverse = theta_base ** (-2.0 * np.arange(HD // 2, dtype=np.float64) / HD)
    inverse = np.concatenate([inverse, inverse])[None, :]
    low = np.arange(ROWS, dtype=np.float64)[:, None] * inverse
    high = np.arange(NZ, dtype=np.float64)[:, None] * ROWS * inverse
    return [t.astype(np.float32) for t in (np.cos(low), np.sin(low), np.cos(high), np.sin(high))]


def per_device(tokens, norm_gain, old_master, route_peer, route_slot, out_weight, doc_lengths):
    pad = ((0, 0), (0, LANES - route_peer.shape[1]))
    vmem = pl.BlockSpec(memory_space=pltpu.VMEM)
    hbm = pl.BlockSpec(memory_space=pl.ANY)
    dma = pltpu.SemaphoreType.DMA
    update, new_master = pl.pallas_call(
        kernel,
        out_shape=(jax.ShapeDtypeStruct((ROWS, D), BF16), jax.ShapeDtypeStruct((96, BLK), F32)),
        in_specs=[hbm, vmem, vmem, vmem, vmem, hbm, pl.BlockSpec(memory_space=pltpu.SMEM)] + [vmem] * 4,
        out_specs=(hbm, hbm),
        scratch_shapes=[
            pltpu.VMEM((ROWS, D), BF16),
            pltpu.VMEM((8 * LANES, 256), BF16),
            pltpu.VMEM((NF * 16, W), BF16),
            pltpu.VMEM((NF * 16, W), BF16),
            pltpu.VMEM((D, W), BF16),
            pltpu.VMEM((2, 16, 512, 256), BF16),
            pltpu.VMEM(((BACK + 1) * ROWS, 256), BF16),
            pltpu.VMEM((ROWS, W), F32),
            pltpu.VMEM((ROWS, QW), BF16),
            pltpu.VMEM((ROWS, D), BF16),
            pltpu.VMEM((96, BLK), F32),
            pltpu.VMEM((ROWS, (BACK + 1) * ROWS), F32),
            dma((3,)),
            dma((NF,)), dma((NF,)),
            dma((80,)), dma((80,)),
            dma((32,)), dma((32,)),
            dma((16,)), dma((16,)),
            dma((8,)), dma((8,)),
            dma((8,)), dma((8,)),
            dma((4,)), dma((4,)),
            dma((4,)),
        ],
        compiler_params=pltpu.CompilerParams(
            collective_id=0, has_side_effects=True, vmem_limit_bytes=56 * 1024 * 1024
        ),
        cost_estimate=pl.CostEstimate(flops=8 * 10**9, bytes_accessed=10**7, transcendentals=1310720),
    )(
        tokens[0],
        norm_gain[None, :],
        old_master,
        jnp.pad(route_peer, pad, constant_values=-1),
        jnp.pad(route_slot, pad, constant_values=-1),
        out_weight,
        doc_lengths,
        *rotation_tables(),
    )
    return (update[None], new_master)


def solution(mesh):
    placed = (
        P("fsdp", "dp", None),
        P(),
        P("fsdp", None),
        P(),
        P(),
        P(None, "fsdp"),
        P("fsdp", None),
    )
    return jax.shard_map(
        per_device,
        mesh=mesh,
        in_specs=placed,
        out_specs=(P("fsdp", "dp", None), P("fsdp", None)),
        check_vma=False,
    )
```

```python
import jax
import jax.numpy as jnp
import numpy as np
from jax import lax
from jax.experimental import pallas as pl
from jax.experimental.pallas import tpu as pltpu
from jax.sharding import PartitionSpec as P

HD = 128
HQ = 4
BLK = 2048
theta_base = 500000.0
epsilon = 1e-05
masked_score = -1e30
MESH = pl.DeviceIdType.MESH
F32, BF16, I32 = jnp.float32, jnp.bfloat16, jnp.int32

NF, NZ = 32, 8
ROWS, D = 256, 8192
QW, KVW, W = 512, 256, 768
LANES = 128
COLS = ((QW, KVW), (0, QW))
OZ = 64
UP, DOWN = 3, 4
PARTS = 4
BACK = 4


def dot(a, b):
    return jnp.dot(a, b, preferred_element_type=F32)


def iota(shape, axis):
    return lax.broadcasted_iota(I32, shape, axis)


def hot(condition):
    return jnp.where(condition, 1.0, 0.0).astype(BF16)


def kernel(
    tok_hbm, gain, old, peer_in, slot_in, ow_hbm, docs, cos_r, sin_r, cos_z, sin_z,
    att, obuf, nm,
    tok, peer, slot, oldb, spread, blocks, sendbuf, inbuf, wbuf, kvbuf, acc, bias,
    local_sem, a2a_s, a2a_r, w_s, w_r, sib_s, sib_r, ow_s, ow_r, oz_s, oz_r, os_s, os_r, kv_s, kv_r,
):
    me = lax.axis_index("fsdp")
    z = lax.axis_index("dp")
    c = lax.rem(me, 2)
    y = lax.rem(lax.div(me, 2), 4)
    x = lax.div(me, 8)
    place = x * 4 + y
    sibling = me + 1 - 2 * c
    up, down = lax.rem(z + 1, NZ), lax.rem(z + NZ - 1, NZ)

    def panel(dx, dy, core):
        return lax.rem(x + 4 - dx, 4) * 8 + lax.rem(y + 4 - dy, 4) * 2 + core

    def remote(src, dst, send, recv, **to):
        return pltpu.make_async_remote_copy(
            src_ref=src, dst_ref=dst, send_sem=send, recv_sem=recv, device_id=to, device_id_type=MESH
        )

    kvbuf[pl.ds(ROWS, BACK * ROWS), :] = jnp.zeros((BACK * ROWS, 256), BF16)

    barrier = pltpu.get_barrier_semaphore()

    @pl.loop(1, NF)
    def _(k):
        pl.semaphore_signal(barrier, inc=1, device_id={"fsdp": lax.rem(me + k, NF)}, device_id_type=MESH)

    for to in (up, down):
        pl.semaphore_signal(barrier, inc=1, device_id={"dp": to}, device_id_type=MESH)

    tokens_in = pltpu.make_async_copy(tok_hbm, tok, local_sem.at[0])
    tokens_in.start()
    own_rows = pl.ds(pl.multiple_of(z * OZ, 16), OZ)
    own_out = pltpu.make_async_copy(ow_hbm.at[own_rows, :], obuf.at[c, place, own_rows, :], local_sem.at[1])
    own_out.start()
    for padded, given in ((peer, peer_in), (slot, slot_in)):
        padded[...] = jnp.full_like(padded, -1)
        padded[:, pl.ds(0, 96)] = given[...]

    for part in range(8):
        oldb[pl.ds(part * LANES, 96), :] = old[:, pl.ds(part * 256, 256)].astype(BF16)
        oldb[pl.ds(part * LANES + 96, 32), :] = jnp.zeros((32, 256), BF16)
    before = hot(iota((LANES, LANES), 0) < iota((LANES, LANES), 1))
    own_peer = peer[pl.ds(me, 1), :]
    mine = iota((NF, LANES), 0) == own_peer
    rank = jnp.sum(jnp.where(mine, dot(hot(mine), before), 0.0), axis=0, keepdims=True).astype(I32)
    pl.semaphore_wait(barrier, NF - 1 + 2)

    def ow_to(k):
        to = lax.rem(place + k, 16)
        return remote(
            ow_hbm.at[own_rows, :], obuf.at[c, place, own_rows, :], ow_s.at[to], ow_r.at[place], fsdp=to * 2 + c
        )

    def ow_from(f):
        return remote(
            ow_hbm.at[own_rows, :], obuf.at[c, f, own_rows, :], ow_s.at[f], ow_r.at[f], fsdp=f * 2 + c
        )

    @pl.loop(1, 16)
    def _(k):
        ow_to(k).start()

    for g in range(3):
        target = jnp.where((own_peer >= 0) & ((rank >> 1) == g), own_peer * 2 + (rank & 1), -1)
        select = hot(iota((NF * 2, LANES), 0) == target)
        for part in range(8):
            block = dot(select, oldb[pl.ds(part * LANES, LANES), :])
            for h in range(2):
                spread[g * 2 + h, pl.ds(part, NF * 2, stride=8), :] = block[:, h * LANES : (h + 1) * LANES]
    for t in range(6):
        sendbuf[:, pl.ds(t * LANES, LANES)] = spread[t].astype(BF16)

    def sixteen(f):
        return pl.ds(pl.multiple_of(f * 16, 16), 16)

    def a2a(to):
        return remote(
            sendbuf.at[sixteen(to), :], inbuf.at[sixteen(me), :], a2a_s.at[to], a2a_r.at[me], fsdp=to
        )

    def a2a_from(f):
        return remote(
            sendbuf.at[sixteen(f), :], inbuf.at[sixteen(f), :], a2a_s.at[f], a2a_r.at[f], fsdp=f
        )

    order = [(dx, dy, dc) for dx in range(4) for dy in range(4) for dc in range(2)][1:]
    for dx, dy, dc in sorted(order, key=lambda t: -(t[0] & 1) - (t[1] & 1) - 2 * (t[0] == 2) - 2 * (t[1] == 2)):
        a2a(panel(dx, dy, 1 - c if dc else c)).start()

    inbuf[sixteen(me), :] = sendbuf[sixteen(me), :]

    def oz_ref(at, core, part):
        rows = pl.ds(pl.multiple_of(lax.rem(at + NZ, NZ) * OZ, 16), OZ)
        return obuf.at[core, pl.ds(part * (16 // PARTS), 16 // PARTS), rows, :]

    def oz(way, step, part, sending):
        hops = step - 1 if sending else step
        ref = oz_ref(z - hops if way == 0 else z + hops, c, part)
        index = (way * UP + step - 1) * PARTS + part
        return remote(ref, ref, oz_s.at[index], oz_r.at[index], dp=up if way == 0 else down)

    def o_side(back, part, core):
        ref = oz_ref(z - back, core, part)
        index = back * PARTS + part
        return remote(ref, ref, os_s.at[index], os_r.at[index], fsdp=sibling)

    def oz_next(step, part):
        if step <= UP:
            oz(0, step, part, False).wait_recv()
            if step < UP:
                oz(0, step + 1, part, True).start()
            o_side(step, part, c).start()
        oz(1, step, part, False).wait_recv()
        if step < DOWN:
            oz(1, step + 1, part, True).start()
        o_side(NZ - step, part, c).start()

    events = iter([(step, part) for step in range(1, DOWN + 1) for part in range(PARTS)])

    def oz_events(count):
        for _ in range(count):
            event = next(events, None)
            if event:
                oz_next(*event)

    @pl.loop(1, 16)
    def _(k):
        ow_from(lax.rem(place + 16 - k, 16)).wait_recv()

    own_out.wait()
    for part in range(PARTS):
        oz(0, 1, part, True).start()
        oz(1, 1, part, True).start()
    for part in range(PARTS):
        o_side(0, part, c).start()

    tokens_in.wait()

    @pl.loop(0, ROWS // 16)
    def _(i):
        rows = pl.ds(pl.multiple_of(i * 16, 16), 16)
        values = tok[rows, :].astype(F32)
        square_mean = jnp.mean(values * values, axis=-1, keepdims=True)
        tok[rows, :] = (values * lax.rsqrt(square_mean + epsilon) * gain[...]).astype(BF16)

    ours = peer[...] == me
    arrival = dot(hot(ours), before)
    holder = iota((NF, NF * 2), 0) == (iota((NF, NF * 2), 1) >> 1)
    odd = (iota((NF, NF * 2), 1) & 1) == 1
    slots = []
    for r in range(6):
        found = ours & (arrival == float(r))
        slots.append(jnp.sum(jnp.where(found, slot[...] + 1, 0), axis=1, keepdims=True) - 1)
    selects = []
    for g in range(3):
        places = jnp.sum(jnp.where(holder, jnp.where(odd, slots[2 * g + 1], slots[2 * g]), 0), axis=0, keepdims=True)
        selects.append(hot(iota((96, NF * 2), 0) == places))

    @pl.loop(1, NF)
    def _(k):
        a2a_from(lax.rem(me + NF - k, NF)).wait_recv()

    def panel_rows(f):
        return pl.ds(pl.multiple_of(f * ROWS, ROWS), ROWS)

    for t in range(6):
        spread[t] = inbuf[:, pl.ds(t * LANES, LANES)].astype(F32)
    for part in range(8):
        for h in range(2):
            total = jnp.zeros((96, LANES), F32)
            for g in range(3):
                piece = spread[g * 2 + h, pl.ds(part, NF * 2, stride=8), :].astype(BF16)
                total += dot(selects[g], piece)
            nm[:, pl.ds((part * 2 + h) * LANES, LANES)] = total
            blocks[part * 2 + h] = total
    for k in range(3):
        for part in range(8):
            row, third = divmod(8 * k + part, 3)
            for h in range(2):
                piece = blocks[part * 2 + h, pl.ds(k, 32, stride=3), :]
                spread[third * 2 + h, pl.ds(row, 32, stride=8), :] = piece
    for t in range(6):
        wbuf[panel_rows(me), pl.ds(t * LANES, LANES)] = spread[t, pl.ds(0, ROWS), :].astype(BF16)

    def coords(half, first, second):
        return (first, second) if half == 0 else (second, first)

    def neighbour(axis, step):
        if axis == 0:
            return lax.rem(x + 4 + step, 4) * 8 + y * 2 + c
        return x * 8 + lax.rem(y + 4 + step, 4) * 2 + c

    def ring(stage, half, phase, kind, sending):
        step = 1 if kind in (0, 2) else -1
        arrives = {0: 1, 1: 3, 2: 2, 3: 2}[kind]
        leaves = {0: 0, 1: 0, 2: 1, 3: 3}[kind]
        along = leaves if sending else arrives
        if phase == 0:
            dx, dy = coords(half, along, 0)
            axis = half
        else:
            dx, dy = coords(half, phase - 1, along)
            axis = 1 - half
        start = panel(dx, dy, c) * ROWS + half * 128 + (64 if kind == 3 else 0)
        size = 64 if kind >= 2 else 128
        first, width = COLS[stage]
        ref = wbuf.at[pl.ds(pl.multiple_of(start, 64), size), pl.ds(first, width)]
        index = ((stage * 2 + half) * 5 + phase) * 4 + kind
        return remote(ref, ref, w_s.at[index], w_r.at[index], fsdp=neighbour(axis, step))

    def go(stage, phase, kinds):
        for kind in kinds:
            for half in range(2):
                ring(stage, half, phase, kind, True).start()

    def come(stage, phase, kinds):
        for kind in kinds:
            for half in range(2):
                ring(stage, half, phase, kind, False).wait_recv()

    def side(stage, dx, dy, core):
        first, width = COLS[stage]
        ref = wbuf.at[panel_rows(panel(dx, dy, core)), pl.ds(first, width)]
        index = stage * 16 + dx * 4 + dy
        return remote(ref, ref, sib_s.at[index], sib_r.at[index], fsdp=sibling)

    def share(stage, places):
        for dx, dy in places:
            side(stage, dx, dy, c).start()

    def multiply(stage, places, other):
        first, width = COLS[stage]
        for dx, dy in places:
            if other:
                side(stage, dx, dy, 1 - c).wait_recv()
            f = panel(dx, dy, 1 - c if other else c)
            columns = pl.ds(first, width)
            acc[:, columns] += dot(tok[:, panel_rows(f)], wbuf[panel_rows(f), columns])

    near = [(0, 0)]
    cross = [(1, 0), (3, 0), (0, 1), (0, 3)]
    corner = [(1, 1), (1, 3), (3, 1), (3, 3)]
    two = [(2, 0), (0, 2)]
    knight = [(1, 2), (3, 2), (2, 1), (2, 3)]
    far = [(2, 2)]

    def open_stage(stage):
        go(stage, 0, (0, 1))
        go(stage, 1, (0, 1))
        share(stage, near)

    def step_one(stage):
        come(stage, 0, (0,))
        go(stage, 0, (2,))
        go(stage, 2, (0, 1))
        come(stage, 0, (1,))
        go(stage, 0, (3,))
        go(stage, 4, (0, 1))

    def step_two(stage):
        come(stage, 1, (0,))
        go(stage, 1, (2,))
        come(stage, 1, (1,))
        go(stage, 1, (3,))
        share(stage, cross)

    def step_three(stage):
        come(stage, 0, (2, 3))
        go(stage, 3, (0, 1))

    def step_four(stage):
        for phase in (2, 4):
            come(stage, phase, (0,))
            go(stage, phase, (2,))
            come(stage, phase, (1,))
            go(stage, phase, (3,))
        share(stage, corner)

    def step_five(stage):
        come(stage, 1, (2, 3))
        share(stage, two)
        come(stage, 3, (0,))
        go(stage, 3, (2,))
        come(stage, 3, (1,))
        go(stage, 3, (3,))

    def step_six(stage):
        come(stage, 2, (2, 3))
        come(stage, 4, (2, 3))
        share(stage, knight)

    def step_seven(stage):
        come(stage, 3, (2, 3))
        share(stage, far)

    def kv(step):
        src = kvbuf.at[pl.ds((step - 1) * ROWS, ROWS), :]
        dst = kvbuf.at[pl.ds(step * ROWS, ROWS), :]
        return remote(src, dst, kv_s.at[step - 1], kv_r.at[step - 1], dp=up)

    def kv_send(step):
        @pl.when((z < NZ - 1) & (z >= step - 1))
        def _():
            kv(step).start()

    def kv_sent(step):
        @pl.when((z < NZ - 1) & (z >= step - 1))
        def _():
            kv(step).wait_send()

    def kv_next(step):
        @pl.when(z >= step)
        def _():
            kv(step).wait_recv()

        if step < BACK:
            kv_send(step + 1)

    open_stage(0)
    acc[...] = jnp.zeros_like(acc)
    oz_events(3)
    step_one(0)
    step_two(0)
    oz_events(2)
    multiply(0, near, False)
    open_stage(1)
    step_three(0)
    multiply(0, near, True)
    step_four(0)
    multiply(0, cross, False)
    oz_events(2)
    step_five(0)
    multiply(0, cross, True)
    multiply(0, corner, False)
    oz_events(1)
    step_one(1)
    step_six(0)
    multiply(0, corner + two, True)
    multiply(0, two + knight, False)
    oz_events(1)
    step_two(1)
    step_seven(0)
    multiply(0, far, False)
    multiply(0, knight, True)
    oz_events(1)
    step_three(1)
    multiply(0, far, True)

    cz, sz = cos_z[pl.ds(z, 1), :], sin_z[pl.ds(z, 1), :]
    cosine = cos_r[...] * cz - sin_r[...] * sz
    sine = sin_r[...] * cz + cos_r[...] * sz
    sine = jnp.where(iota((ROWS, HD), 1) < HD // 2, -sine, sine)

    def rotate(values):
        return (values * cosine + pltpu.roll(values, HD // 2, 1) * sine).astype(BF16)

    kvbuf[pl.ds(0, ROWS), pl.ds(0, HD)] = rotate(acc[:, pl.ds(QW, HD)])
    kvbuf[pl.ds(0, ROWS), pl.ds(HD, HD)] = acc[:, pl.ds(QW + HD, HD)].astype(BF16)
    kv_send(1)
    oz_events(1)
    step_four(1)
    oz_events(1)
    multiply(1, near + cross, False)
    kv_next(1)
    step_five(1)
    oz_events(1)
    multiply(1, near + cross, True)
    kv_next(2)
    oz_events(1)
    multiply(1, corner + two, False)
    step_six(1)
    oz_events(1)
    multiply(1, corner + two, True)
    kv_next(3)

    query = z * ROWS + iota((ROWS, 1), 0)
    begin = jnp.zeros((ROWS, 1), I32)
    end = jnp.int32(0)
    for d in range(8):
        end = end + docs[0, d]
        begin = jnp.where(query >= end, end, begin)
    for back in range(BACK + 1):
        key = (z - back) * ROWS + iota((ROWS, ROWS), 1)
        bias[:, pl.ds(back * ROWS, ROWS)] = jnp.where((key <= query) & (key >= begin), 0.0, masked_score)

    multiply(1, knight, False)
    step_seven(1)
    multiply(1, knight, True)
    multiply(1, far, False)
    oz_events(1)
    multiply(1, far, True)
    kv_next(4)

    scale = np.float32(np.log2(np.e) / np.sqrt(HD))
    for h in range(HQ):
        columns = pl.ds(h * HD, HD)
        queries = rotate(acc[:, columns])
        scores = lax.dot_general(
            queries, kvbuf[:, pl.ds(0, HD)], (((1,), (1,)), ((), ())), preferred_element_type=F32
        )
        scores = scores * scale + bias[...]
        expterm = jnp.exp2(scores - jnp.max(scores, axis=1, keepdims=True))
        denom = jnp.sum(expterm, axis=1, keepdims=True)
        att[:, columns] = (dot(expterm.astype(BF16), kvbuf[:, pl.ds(HD, HD)]) / denom).astype(BF16)
        oz_events(1)

    for event in events:
        oz_next(*event)
    for part in range(PARTS):
        for back in range(NZ):
            o_side(back, part, 1 - c).wait_recv()

    @pl.loop(1, NF)
    def _(k):
        a2a(lax.rem(me + k, NF)).wait_send()

    @pl.loop(1, 16)
    def _(k):
        ow_to(k).wait_send()

    for stage in range(2):
        for phase in range(5):
            for kind in range(4):
                for half in range(2):
                    ring(stage, half, phase, kind, True).wait_send()
        for dx in range(4):
            for dy in range(4):
                side(stage, dx, dy, c).wait_send()
    for part in range(PARTS):
        for step in range(1, UP + 1):
            oz(0, step, part, True).wait_send()
        for step in range(1, DOWN + 1):
            oz(1, step, part, True).wait_send()
        for back in range(NZ):
            o_side(back, part, c).wait_send()
    for step in range(1, BACK + 1):
        kv_sent(step)


def project(att, weight, nm_in, out, nm, staged, sem):
    routed = pltpu.make_async_copy(nm_in, nm, sem.at[8])
    routed.start()
    copies = [routed]
    for part in range(8):
        for f in range(part * 4, part * 4 + 4):
            staged[:, pl.ds(f * 256, 256)] = dot(att[...], weight[f % 2, f // 2]).astype(BF16)
        columns = pl.ds(part * 1024, 1024)
        copies.append(pltpu.make_async_copy(staged.at[:, columns], out.at[:, columns], sem.at[part]))
        copies[-1].start()
    for copy in copies:
        copy.wait()


def rotation_tables():
    inverse = theta_base ** (-2.0 * np.arange(HD // 2, dtype=np.float64) / HD)
    inverse = np.concatenate([inverse, inverse])[None, :]
    low = np.arange(ROWS, dtype=np.float64)[:, None] * inverse
    high = np.arange(NZ, dtype=np.float64)[:, None] * ROWS * inverse
    return [t.astype(np.float32) for t in (np.cos(low), np.sin(low), np.cos(high), np.sin(high))]


def per_device(tokens, norm_gain, old_master, route_peer, route_slot, out_weight, doc_lengths):
    vmem = pl.BlockSpec(memory_space=pltpu.VMEM)
    hbm = pl.BlockSpec(memory_space=pl.ANY)
    dma = pltpu.SemaphoreType.DMA
    attended, gathered, routed = pl.pallas_call(
        kernel,
        out_shape=(
            pltpu.VMEM((ROWS, QW), BF16),
            pltpu.VMEM((2, 16, 512, 256), BF16),
            pltpu.VMEM((96, BLK), F32),
        ),
        in_specs=[hbm, vmem, vmem, vmem, vmem, hbm, pl.BlockSpec(memory_space=pltpu.SMEM)] + [vmem] * 4,
        out_specs=(vmem, vmem, vmem),
        scratch_shapes=[
            pltpu.VMEM((ROWS, D), BF16),
            pltpu.VMEM((NF, LANES), I32),
            pltpu.VMEM((NF, LANES), I32),
            pltpu.VMEM((8 * LANES, 256), BF16),
            pltpu.VMEM((6, NF * 16, LANES), F32),
            pltpu.VMEM((16, 96, LANES), F32),
            pltpu.VMEM((NF * 16, W), BF16),
            pltpu.VMEM((NF * 16, W), BF16),
            pltpu.VMEM((D, W), BF16),
            pltpu.VMEM(((BACK + 1) * ROWS, 256), BF16),
            pltpu.VMEM((ROWS, W), F32),
            pltpu.VMEM((ROWS, (BACK + 1) * ROWS), F32),
            dma((3,)),
            dma((NF,)), dma((NF,)),
            dma((80,)), dma((80,)),
            dma((32,)), dma((32,)),
            dma((16,)), dma((16,)),
            dma(((UP + DOWN) * PARTS,)), dma(((UP + DOWN) * PARTS,)),
            dma((NZ * PARTS,)), dma((NZ * PARTS,)),
            dma((4,)), dma((4,)),
        ],
        compiler_params=pltpu.CompilerParams(
            collective_id=0, has_side_effects=True, vmem_limit_bytes=50 * 1024 * 1024
        ),
        cost_estimate=pl.CostEstimate(flops=8 * 10**9, bytes_accessed=10**7, transcendentals=1310720),
    )(
        tokens[0],
        norm_gain[None, :],
        old_master,
        route_peer,
        route_slot,
        out_weight,
        doc_lengths,
        *rotation_tables(),
    )
    update, new_master = pl.pallas_call(
        project,
        out_shape=(jax.ShapeDtypeStruct((ROWS, D), BF16), jax.ShapeDtypeStruct((96, BLK), F32)),
        in_specs=[vmem, vmem, vmem],
        out_specs=(hbm, hbm),
        scratch_shapes=[pltpu.VMEM((ROWS, D), BF16), dma((9,))],
        compiler_params=pltpu.CompilerParams(vmem_limit_bytes=16 * 1024 * 1024),
        cost_estimate=pl.CostEstimate(flops=2 * ROWS * QW * D, bytes_accessed=5 * 10**6, transcendentals=0),
    )(attended, gathered, routed)
    return (update[None], new_master)


def solution(mesh):
    placed = (
        P("fsdp", "dp", None),
        P(),
        P("fsdp", None),
        P(),
        P(),
        P(None, "fsdp"),
        P("fsdp", None),
    )
    return jax.shard_map(
        per_device,
        mesh=mesh,
        in_specs=placed,
        out_specs=(P("fsdp", "dp", None), P("fsdp", None)),
        check_vma=False,
    )
```

```python
import jax
import jax.numpy as jnp
import numpy as np
from jax import lax
from jax.experimental import pallas as pl
from jax.experimental.pallas import tpu as pltpu
from jax.sharding import PartitionSpec as P

HD = 128
HQ = 4
BLK = 2048
theta_base = 500000.0
epsilon = 1e-05
masked_score = -1e30
MESH = pl.DeviceIdType.MESH
F32, BF16, I32 = jnp.float32, jnp.bfloat16, jnp.int32

NF, NZ = 32, 8
ROWS, D = 256, 8192
QW, KVW, W = 512, 256, 768
LANES = 128
COLS = ((QW, KVW), (0, QW))
OZ = 64
UP, DOWN = 3, 4
PARTS = 4
BACK = 4


def dot(a, b):
    return jnp.dot(a, b, preferred_element_type=F32)


def iota(shape, axis):
    return lax.broadcasted_iota(I32, shape, axis)


def hot(condition):
    return jnp.where(condition, 1.0, 0.0).astype(BF16)


def kernel(
    tok_hbm, gain, old, peer_in, slot_in, ow_hbm, docs, cos_r, sin_r, cos_z, sin_z,
    att, obuf, nm,
    tok, peer, slot, oldb, spread, blocks, sendbuf, inbuf, wbuf, kvbuf, acc, bias,
    local_sem, a2a_s, a2a_r, w_s, w_r, sib_s, sib_r, ow_s, ow_r, oz_s, oz_r, os_s, os_r, kv_s, kv_r,
):
    me = lax.axis_index("fsdp")
    z = lax.axis_index("dp")
    c = lax.rem(me, 2)
    y = lax.rem(lax.div(me, 2), 4)
    x = lax.div(me, 8)
    place = x * 4 + y
    sibling = me + 1 - 2 * c
    up, down = lax.rem(z + 1, NZ), lax.rem(z + NZ - 1, NZ)

    def panel(dx, dy, core):
        return lax.rem(x + 4 - dx, 4) * 8 + lax.rem(y + 4 - dy, 4) * 2 + core

    def remote(src, dst, send, recv, **to):
        return pltpu.make_async_remote_copy(
            src_ref=src, dst_ref=dst, send_sem=send, recv_sem=recv, device_id=to, device_id_type=MESH
        )

    kvbuf[pl.ds(ROWS, BACK * ROWS), :] = jnp.zeros((BACK * ROWS, 256), BF16)

    barrier = pltpu.get_barrier_semaphore()

    @pl.loop(1, NF)
    def _(k):
        pl.semaphore_signal(barrier, inc=1, device_id={"fsdp": lax.rem(me + k, NF)}, device_id_type=MESH)

    for to in (up, down):
        pl.semaphore_signal(barrier, inc=1, device_id={"dp": to}, device_id_type=MESH)

    tokens_in = pltpu.make_async_copy(tok_hbm, tok, local_sem.at[0])
    tokens_in.start()
    own_rows = pl.ds(pl.multiple_of(z * OZ, 16), OZ)
    own_out = pltpu.make_async_copy(ow_hbm.at[own_rows, :], obuf.at[c, place, own_rows, :], local_sem.at[1])
    own_out.start()
    for padded, given in ((peer, peer_in), (slot, slot_in)):
        padded[...] = jnp.full_like(padded, -1)
        padded[:, pl.ds(0, 96)] = given[...]

    for part in range(8):
        oldb[pl.ds(part * LANES, 96), :] = old[:, pl.ds(part * 256, 256)].astype(BF16)
        oldb[pl.ds(part * LANES + 96, 32), :] = jnp.zeros((32, 256), BF16)
    before = hot(iota((LANES, LANES), 0) < iota((LANES, LANES), 1))
    own_peer = peer[pl.ds(me, 1), :]
    mine = iota((NF, LANES), 0) == own_peer
    rank = jnp.sum(jnp.where(mine, dot(hot(mine), before), 0.0), axis=0, keepdims=True).astype(I32)
    pl.semaphore_wait(barrier, NF - 1 + 2)

    def ow_to(k):
        to = lax.rem(place + k, 16)
        return remote(
            ow_hbm.at[own_rows, :], obuf.at[c, place, own_rows, :], ow_s.at[to], ow_r.at[place], fsdp=to * 2 + c
        )

    def ow_from(f):
        return remote(
            ow_hbm.at[own_rows, :], obuf.at[c, f, own_rows, :], ow_s.at[f], ow_r.at[f], fsdp=f * 2 + c
        )

    @pl.loop(1, 16)
    def _(k):
        ow_to(k).start()

    for g in range(3):
        target = jnp.where((own_peer >= 0) & ((rank >> 1) == g), own_peer * 2 + (rank & 1), -1)
        select = hot(iota((NF * 2, LANES), 0) == target)
        for part in range(8):
            block = dot(select, oldb[pl.ds(part * LANES, LANES), :])
            for h in range(2):
                spread[g * 2 + h, pl.ds(part, NF * 2, stride=8), :] = block[:, h * LANES : (h + 1) * LANES]
    for t in range(6):
        sendbuf[:, pl.ds(t * LANES, LANES)] = spread[t].astype(BF16)

    def sixteen(f):
        return pl.ds(pl.multiple_of(f * 16, 16), 16)

    def a2a(to):
        return remote(
            sendbuf.at[sixteen(to), :], inbuf.at[sixteen(me), :], a2a_s.at[to], a2a_r.at[me], fsdp=to
        )

    def a2a_from(f):
        return remote(
            sendbuf.at[sixteen(f), :], inbuf.at[sixteen(f), :], a2a_s.at[f], a2a_r.at[f], fsdp=f
        )

    order = [(dx, dy, dc) for dx in range(4) for dy in range(4) for dc in range(2)][1:]
    for dx, dy, dc in sorted(order, key=lambda t: -(t[0] & 1) - (t[1] & 1) - 2 * (t[0] == 2) - 2 * (t[1] == 2)):
        a2a(panel(dx, dy, 1 - c if dc else c)).start()

    inbuf[sixteen(me), :] = sendbuf[sixteen(me), :]

    def oz_ref(at, core, part):
        rows = pl.ds(pl.multiple_of(lax.rem(at + NZ, NZ) * OZ, 16), OZ)
        return obuf.at[core, pl.ds(part * (16 // PARTS), 16 // PARTS), rows, :]

    def oz(way, step, part, sending):
        hops = step - 1 if sending else step
        ref = oz_ref(z - hops if way == 0 else z + hops, c, part)
        index = (way * UP + step - 1) * PARTS + part
        return remote(ref, ref, oz_s.at[index], oz_r.at[index], dp=up if way == 0 else down)

    def o_side(back, part, core):
        ref = oz_ref(z - back, core, part)
        index = back * PARTS + part
        return remote(ref, ref, os_s.at[index], os_r.at[index], fsdp=sibling)

    def oz_next(step, part):
        if step <= UP:
            oz(0, step, part, False).wait_recv()
            if step < UP:
                oz(0, step + 1, part, True).start()
            o_side(step, part, c).start()
        oz(1, step, part, False).wait_recv()
        if step < DOWN:
            oz(1, step + 1, part, True).start()
        o_side(NZ - step, part, c).start()

    events = iter([(step, part) for step in range(1, DOWN + 1) for part in range(PARTS)])

    def oz_events(count):
        for _ in range(count):
            event = next(events, None)
            if event:
                oz_next(*event)

    @pl.loop(1, 16)
    def _(k):
        ow_from(lax.rem(place + 16 - k, 16)).wait_recv()

    own_out.wait()
    for part in range(PARTS):
        oz(0, 1, part, True).start()
        oz(1, 1, part, True).start()
    for part in range(PARTS):
        o_side(0, part, c).start()

    tokens_in.wait()

    @pl.loop(0, ROWS // 16)
    def _(i):
        rows = pl.ds(pl.multiple_of(i * 16, 16), 16)
        values = tok[rows, :].astype(F32)
        square_mean = jnp.mean(values * values, axis=-1, keepdims=True)
        tok[rows, :] = (values * lax.rsqrt(square_mean + epsilon) * gain[...]).astype(BF16)

    query = z * ROWS + iota((ROWS, 1), 0)
    begin = jnp.zeros((ROWS, 1), I32)
    end = jnp.int32(0)
    for d in range(8):
        end = end + docs[0, d]
        begin = jnp.where(query >= end, end, begin)
    for back in range(BACK + 1):
        key = (z - back) * ROWS + iota((ROWS, ROWS), 1)
        bias[:, pl.ds(back * ROWS, ROWS)] = jnp.where((key <= query) & (key >= begin), 0.0, masked_score)

    ours = peer[...] == me
    arrival = dot(hot(ours), before)
    holder = iota((NF, NF * 2), 0) == (iota((NF, NF * 2), 1) >> 1)
    odd = (iota((NF, NF * 2), 1) & 1) == 1
    slots = []
    for r in range(6):
        found = ours & (arrival == float(r))
        slots.append(jnp.sum(jnp.where(found, slot[...] + 1, 0), axis=1, keepdims=True) - 1)
    selects = []
    for g in range(3):
        places = jnp.sum(jnp.where(holder, jnp.where(odd, slots[2 * g + 1], slots[2 * g]), 0), axis=0, keepdims=True)
        selects.append(hot(iota((96, NF * 2), 0) == places))

    @pl.loop(1, NF)
    def _(k):
        a2a_from(lax.rem(me + NF - k, NF)).wait_recv()

    def panel_rows(f):
        return pl.ds(pl.multiple_of(f * ROWS, ROWS), ROWS)

    for t in range(6):
        spread[t] = inbuf[:, pl.ds(t * LANES, LANES)].astype(F32)
    for part in range(8):
        for h in range(2):
            total = jnp.zeros((96, LANES), F32)
            for g in range(3):
                piece = spread[g * 2 + h, pl.ds(part, NF * 2, stride=8), :].astype(BF16)
                total += dot(selects[g], piece)
            nm[:, pl.ds((part * 2 + h) * LANES, LANES)] = total
            blocks[part * 2 + h] = total
    for k in range(3):
        for part in range(8):
            row, third = divmod(8 * k + part, 3)
            for h in range(2):
                piece = blocks[part * 2 + h, pl.ds(k, 32, stride=3), :]
                spread[third * 2 + h, pl.ds(row, 32, stride=8), :] = piece
    for t in range(6):
        wbuf[panel_rows(me), pl.ds(t * LANES, LANES)] = spread[t, pl.ds(0, ROWS), :].astype(BF16)

    def coords(half, first, second):
        return (first, second) if half == 0 else (second, first)

    def neighbour(axis, step):
        if axis == 0:
            return lax.rem(x + 4 + step, 4) * 8 + y * 2 + c
        return x * 8 + lax.rem(y + 4 + step, 4) * 2 + c

    def ring(stage, half, phase, kind, sending):
        step = 1 if kind in (0, 2) else -1
        arrives = {0: 1, 1: 3, 2: 2, 3: 2}[kind]
        leaves = {0: 0, 1: 0, 2: 1, 3: 3}[kind]
        along = leaves if sending else arrives
        if phase == 0:
            dx, dy = coords(half, along, 0)
            axis = half
        else:
            dx, dy = coords(half, phase - 1, along)
            axis = 1 - half
        start = panel(dx, dy, c) * ROWS + half * 128 + (64 if kind == 3 else 0)
        size = 64 if kind >= 2 else 128
        first, width = COLS[stage]
        ref = wbuf.at[pl.ds(pl.multiple_of(start, 64), size), pl.ds(first, width)]
        index = ((stage * 2 + half) * 5 + phase) * 4 + kind
        return remote(ref, ref, w_s.at[index], w_r.at[index], fsdp=neighbour(axis, step))

    def go(stage, phase, kinds):
        for kind in kinds:
            for half in range(2):
                ring(stage, half, phase, kind, True).start()

    def come(stage, phase, kinds):
        for kind in kinds:
            for half in range(2):
                ring(stage, half, phase, kind, False).wait_recv()

    def side(stage, dx, dy, core):
        first, width = COLS[stage]
        ref = wbuf.at[panel_rows(panel(dx, dy, core)), pl.ds(first, width)]
        index = stage * 16 + dx * 4 + dy
        return remote(ref, ref, sib_s.at[index], sib_r.at[index], fsdp=sibling)

    def share(stage, places):
        for dx, dy in places:
            side(stage, dx, dy, c).start()

    def multiply(stage, places, other):
        first, width = COLS[stage]
        columns = pl.ds(first, width)
        if other:
            for dx, dy in places:
                side(stage, dx, dy, 1 - c).wait_recv()
        rows = [panel_rows(panel(dx, dy, 1 - c if other else c)) for dx, dy in places]
        left = jnp.concatenate([tok[:, r] for r in rows], axis=1)
        right = jnp.concatenate([wbuf[r, columns] for r in rows], axis=0)
        acc[:, columns] += dot(left, right)

    near = [(0, 0)]
    cross = [(1, 0), (3, 0), (0, 1), (0, 3)]
    corner = [(1, 1), (1, 3), (3, 1), (3, 3)]
    two = [(2, 0), (0, 2)]
    knight = [(1, 2), (3, 2), (2, 1), (2, 3)]
    far = [(2, 2)]

    def open_stage(stage):
        go(stage, 0, (0, 1))
        go(stage, 1, (0, 1))
        share(stage, near)

    def step_one(stage):
        come(stage, 0, (0,))
        go(stage, 0, (2,))
        go(stage, 2, (0, 1))
        come(stage, 0, (1,))
        go(stage, 0, (3,))
        go(stage, 4, (0, 1))

    def step_two(stage):
        come(stage, 1, (0,))
        go(stage, 1, (2,))
        come(stage, 1, (1,))
        go(stage, 1, (3,))
        share(stage, cross)

    def step_three(stage):
        come(stage, 0, (2, 3))
        go(stage, 3, (0, 1))

    def step_four(stage):
        for phase in (2, 4):
            come(stage, phase, (0,))
            go(stage, phase, (2,))
            come(stage, phase, (1,))
            go(stage, phase, (3,))
        share(stage, corner)

    def step_five(stage):
        come(stage, 1, (2, 3))
        share(stage, two)
        come(stage, 3, (0,))
        go(stage, 3, (2,))
        come(stage, 3, (1,))
        go(stage, 3, (3,))

    def step_six(stage):
        come(stage, 2, (2, 3))
        come(stage, 4, (2, 3))
        share(stage, knight)

    def step_seven(stage):
        come(stage, 3, (2, 3))
        share(stage, far)

    def kv(step):
        src = kvbuf.at[pl.ds((step - 1) * ROWS, ROWS), :]
        dst = kvbuf.at[pl.ds(step * ROWS, ROWS), :]
        return remote(src, dst, kv_s.at[step - 1], kv_r.at[step - 1], dp=up)

    def kv_send(step):
        @pl.when((z < NZ - 1) & (z >= step - 1))
        def _():
            kv(step).start()

    def kv_sent(step):
        @pl.when((z < NZ - 1) & (z >= step - 1))
        def _():
            kv(step).wait_send()

    def kv_next(step):
        @pl.when(z >= step)
        def _():
            kv(step).wait_recv()

        if step < BACK:
            kv_send(step + 1)

    open_stage(0)
    acc[...] = jnp.zeros_like(acc)
    oz_events(2)
    step_one(0)
    oz_events(1)
    step_two(0)
    oz_events(1)
    multiply(0, near, False)
    open_stage(1)
    step_three(0)
    multiply(0, near, True)
    step_four(0)
    oz_events(1)
    multiply(0, cross, False)
    oz_events(1)
    step_five(0)
    multiply(0, cross, True)
    multiply(0, corner, False)
    oz_events(1)
    step_one(1)
    step_six(0)
    multiply(0, corner + two, True)
    multiply(0, two + knight, False)
    oz_events(1)
    step_two(1)
    step_seven(0)
    multiply(0, knight, True)
    multiply(0, far, False)
    oz_events(1)
    step_three(1)
    multiply(0, far, True)

    cz, sz = cos_z[pl.ds(z, 1), :], sin_z[pl.ds(z, 1), :]
    cosine = cos_r[...] * cz - sin_r[...] * sz
    sine = sin_r[...] * cz + cos_r[...] * sz
    sine = jnp.where(iota((ROWS, HD), 1) < HD // 2, -sine, sine)

    def rotate(values):
        return (values * cosine + pltpu.roll(values, HD // 2, 1) * sine).astype(BF16)

    kvbuf[pl.ds(0, ROWS), pl.ds(0, HD)] = rotate(acc[:, pl.ds(QW, HD)])
    kvbuf[pl.ds(0, ROWS), pl.ds(HD, HD)] = acc[:, pl.ds(QW + HD, HD)].astype(BF16)
    kv_send(1)
    multiply(1, near + cross, False)
    oz_events(1)
    step_four(1)
    multiply(1, near + cross, True)
    oz_events(1)
    multiply(1, corner, False)
    kv_next(1)
    step_five(1)
    oz_events(1)
    multiply(1, corner, True)
    multiply(1, two, False)
    kv_next(2)
    oz_events(1)
    step_six(1)
    multiply(1, knight, False)
    multiply(1, two, True)
    oz_events(1)
    kv_next(3)
    step_seven(1)
    multiply(1, knight, True)
    oz_events(1)
    multiply(1, far, False)
    multiply(1, far, True)
    kv_next(4)

    scale = np.float32(np.log2(np.e) / np.sqrt(HD))
    for h in range(HQ):
        columns = pl.ds(h * HD, HD)
        queries = rotate(acc[:, columns])
        scores = lax.dot_general(
            queries, kvbuf[:, pl.ds(0, HD)], (((1,), (1,)), ((), ())), preferred_element_type=F32
        )
        scores = scores * scale + bias[...]
        expterm = jnp.exp2(scores - jnp.max(scores, axis=1, keepdims=True))
        denom = jnp.sum(expterm, axis=1, keepdims=True)
        att[:, columns] = (dot(expterm.astype(BF16), kvbuf[:, pl.ds(HD, HD)]) / denom).astype(BF16)
        oz_events(1)

    for event in events:
        oz_next(*event)
    for part in range(PARTS):
        for back in range(NZ):
            o_side(back, part, 1 - c).wait_recv()

    @pl.loop(1, NF)
    def _(k):
        a2a(lax.rem(me + k, NF)).wait_send()

    @pl.loop(1, 16)
    def _(k):
        ow_to(k).wait_send()

    for stage in range(2):
        for phase in range(5):
            for kind in range(4):
                for half in range(2):
                    ring(stage, half, phase, kind, True).wait_send()
        for dx in range(4):
            for dy in range(4):
                side(stage, dx, dy, c).wait_send()
    for part in range(PARTS):
        for step in range(1, UP + 1):
            oz(0, step, part, True).wait_send()
        for step in range(1, DOWN + 1):
            oz(1, step, part, True).wait_send()
        for back in range(NZ):
            o_side(back, part, c).wait_send()
    for step in range(1, BACK + 1):
        kv_sent(step)


def project(att, weight, nm_in, out, nm, staged, sem):
    routed = pltpu.make_async_copy(nm_in, nm, sem.at[8])
    routed.start()
    copies = [routed]
    for part in range(8):
        for f in range(part * 4, part * 4 + 4):
            staged[:, pl.ds(f * 256, 256)] = dot(att[...], weight[f % 2, f // 2]).astype(BF16)
        columns = pl.ds(part * 1024, 1024)
        copies.append(pltpu.make_async_copy(staged.at[:, columns], out.at[:, columns], sem.at[part]))
        copies[-1].start()
    for copy in copies:
        copy.wait()


def rotation_tables():
    inverse = theta_base ** (-2.0 * np.arange(HD // 2, dtype=np.float64) / HD)
    inverse = np.concatenate([inverse, inverse])[None, :]
    low = np.arange(ROWS, dtype=np.float64)[:, None] * inverse
    high = np.arange(NZ, dtype=np.float64)[:, None] * ROWS * inverse
    return [t.astype(np.float32) for t in (np.cos(low), np.sin(low), np.cos(high), np.sin(high))]


def per_device(tokens, norm_gain, old_master, route_peer, route_slot, out_weight, doc_lengths):
    vmem = pl.BlockSpec(memory_space=pltpu.VMEM)
    hbm = pl.BlockSpec(memory_space=pl.ANY)
    dma = pltpu.SemaphoreType.DMA
    attended, gathered, routed = pl.pallas_call(
        kernel,
        out_shape=(
            pltpu.VMEM((ROWS, QW), BF16),
            pltpu.VMEM((2, 16, 512, 256), BF16),
            pltpu.VMEM((96, BLK), F32),
        ),
        in_specs=[hbm, vmem, vmem, vmem, vmem, hbm, pl.BlockSpec(memory_space=pltpu.SMEM)] + [vmem] * 4,
        out_specs=(vmem, vmem, vmem),
        scratch_shapes=[
            pltpu.VMEM((ROWS, D), BF16),
            pltpu.VMEM((NF, LANES), I32),
            pltpu.VMEM((NF, LANES), I32),
            pltpu.VMEM((8 * LANES, 256), BF16),
            pltpu.VMEM((6, NF * 16, LANES), F32),
            pltpu.VMEM((16, 96, LANES), F32),
            pltpu.VMEM((NF * 16, W), BF16),
            pltpu.VMEM((NF * 16, W), BF16),
            pltpu.VMEM((D, W), BF16),
            pltpu.VMEM(((BACK + 1) * ROWS, 256), BF16),
            pltpu.VMEM((ROWS, W), F32),
            pltpu.VMEM((ROWS, (BACK + 1) * ROWS), F32),
            dma((3,)),
            dma((NF,)), dma((NF,)),
            dma((80,)), dma((80,)),
            dma((32,)), dma((32,)),
            dma((16,)), dma((16,)),
            dma(((UP + DOWN) * PARTS,)), dma(((UP + DOWN) * PARTS,)),
            dma((NZ * PARTS,)), dma((NZ * PARTS,)),
            dma((4,)), dma((4,)),
        ],
        compiler_params=pltpu.CompilerParams(
            collective_id=0, has_side_effects=True, vmem_limit_bytes=50 * 1024 * 1024
        ),
        cost_estimate=pl.CostEstimate(flops=8 * 10**9, bytes_accessed=10**7, transcendentals=1310720),
    )(
        tokens[0],
        norm_gain[None, :],
        old_master,
        route_peer,
        route_slot,
        out_weight,
        doc_lengths,
        *rotation_tables(),
    )
    update, new_master = pl.pallas_call(
        project,
        out_shape=(jax.ShapeDtypeStruct((ROWS, D), BF16), jax.ShapeDtypeStruct((96, BLK), F32)),
        in_specs=[vmem, vmem, vmem],
        out_specs=(hbm, hbm),
        scratch_shapes=[pltpu.VMEM((ROWS, D), BF16), dma((9,))],
        compiler_params=pltpu.CompilerParams(vmem_limit_bytes=16 * 1024 * 1024),
        cost_estimate=pl.CostEstimate(flops=2 * ROWS * QW * D, bytes_accessed=5 * 10**6, transcendentals=0),
    )(attended, gathered, routed)
    return (update[None], new_master)


def solution(mesh):
    placed = (
        P("fsdp", "dp", None),
        P(),
        P("fsdp", None),
        P(),
        P(),
        P(None, "fsdp"),
        P("fsdp", None),
    )
    return jax.shard_map(
        per_device,
        mesh=mesh,
        in_specs=placed,
        out_specs=(P("fsdp", "dp", None), P("fsdp", None)),
        check_vma=False,
    )
```

```python
import jax
import jax.numpy as jnp
import numpy as np
from jax import lax
from jax.experimental import pallas as pl
from jax.experimental.pallas import tpu as pltpu
from jax.sharding import PartitionSpec as P

HD = 128
HQ = 4
BLK = 2048
theta_base = 500000.0
epsilon = 1e-05
masked_score = -1e30
MESH = pl.DeviceIdType.MESH
F32, BF16, I32 = jnp.float32, jnp.bfloat16, jnp.int32

NF, NZ = 32, 8
ROWS, D = 256, 8192
QW, KVW, W = 512, 256, 768
LANES = 128
COLS = ((QW, KVW), (0, QW))
OZ = 64
UP, DOWN = 3, 4
PARTS = 4
BACK = 4


def dot(a, b):
    return jnp.dot(a, b, preferred_element_type=F32)


def iota(shape, axis):
    return lax.broadcasted_iota(I32, shape, axis)


def hot(condition):
    return jnp.where(condition, 1.0, 0.0).astype(BF16)


def kernel(
    tok_hbm, gain, old, peer_in, slot_in, ow_hbm, docs, cos_r, sin_r, cos_z, sin_z,
    att, obuf, nm,
    tok, peer, slot, oldb, spread, blocks, sendbuf, inbuf, wbuf, kvbuf, acc, bias,
    local_sem, a2a_s, a2a_r, w_s, w_r, sib_s, sib_r, ow_s, ow_r, oz_s, oz_r, os_s, os_r, kv_s, kv_r,
):
    me = lax.axis_index("fsdp")
    z = lax.axis_index("dp")
    c = lax.rem(me, 2)
    y = lax.rem(lax.div(me, 2), 4)
    x = lax.div(me, 8)
    place = x * 4 + y
    sibling = me + 1 - 2 * c
    up, down = lax.rem(z + 1, NZ), lax.rem(z + NZ - 1, NZ)

    def panel(dx, dy, core):
        return lax.rem(x + 4 - dx, 4) * 8 + lax.rem(y + 4 - dy, 4) * 2 + core

    def remote(src, dst, send, recv, **to):
        return pltpu.make_async_remote_copy(
            src_ref=src, dst_ref=dst, send_sem=send, recv_sem=recv, device_id=to, device_id_type=MESH
        )

    kvbuf[pl.ds(ROWS, BACK * ROWS), :] = jnp.zeros((BACK * ROWS, 256), BF16)

    barrier = pltpu.get_barrier_semaphore()

    @pl.loop(1, NF)
    def _(k):
        pl.semaphore_signal(barrier, inc=1, device_id={"fsdp": lax.rem(me + k, NF)}, device_id_type=MESH)

    for to in (up, down):
        pl.semaphore_signal(barrier, inc=1, device_id={"dp": to}, device_id_type=MESH)

    tokens_in = pltpu.make_async_copy(tok_hbm, tok, local_sem.at[0])
    tokens_in.start()
    own_rows = pl.ds(pl.multiple_of(z * OZ, 16), OZ)
    own_out = pltpu.make_async_copy(ow_hbm.at[own_rows, :], obuf.at[c, place, own_rows, :], local_sem.at[1])
    own_out.start()
    for padded, given in ((peer, peer_in), (slot, slot_in)):
        padded[...] = jnp.full_like(padded, -1)
        padded[:, pl.ds(0, 96)] = given[...]

    for part in range(8):
        oldb[pl.ds(part * LANES, 96), :] = old[:, pl.ds(part * 256, 256)].astype(BF16)
        oldb[pl.ds(part * LANES + 96, 32), :] = jnp.zeros((32, 256), BF16)
    before = hot(iota((LANES, LANES), 0) < iota((LANES, LANES), 1))
    own_peer = peer[pl.ds(me, 1), :]
    mine = iota((NF, LANES), 0) == own_peer
    rank = jnp.sum(jnp.where(mine, dot(hot(mine), before), 0.0), axis=0, keepdims=True).astype(I32)
    pl.semaphore_wait(barrier, NF - 1 + 2)

    def ow_to(k):
        to = lax.rem(place + k, 16)
        return remote(
            ow_hbm.at[own_rows, :], obuf.at[c, place, own_rows, :], ow_s.at[to], ow_r.at[place], fsdp=to * 2 + c
        )

    def ow_from(f):
        return remote(
            ow_hbm.at[own_rows, :], obuf.at[c, f, own_rows, :], ow_s.at[f], ow_r.at[f], fsdp=f * 2 + c
        )

    @pl.loop(1, 16)
    def _(k):
        ow_to(k).start()

    for g in range(3):
        target = jnp.where((own_peer >= 0) & ((rank >> 1) == g), own_peer * 2 + (rank & 1), -1)
        select = hot(iota((NF * 2, LANES), 0) == target)
        for part in range(8):
            block = dot(select, oldb[pl.ds(part * LANES, LANES), :])
            for h in range(2):
                spread[g * 2 + h, pl.ds(part, NF * 2, stride=8), :] = block[:, h * LANES : (h + 1) * LANES]
    for t in range(6):
        sendbuf[:, pl.ds(t * LANES, LANES)] = spread[t].astype(BF16)

    def sixteen(f):
        return pl.ds(pl.multiple_of(f * 16, 16), 16)

    def a2a(to):
        return remote(
            sendbuf.at[sixteen(to), :], inbuf.at[sixteen(me), :], a2a_s.at[to], a2a_r.at[me], fsdp=to
        )

    def a2a_from(f):
        return remote(
            sendbuf.at[sixteen(f), :], inbuf.at[sixteen(f), :], a2a_s.at[f], a2a_r.at[f], fsdp=f
        )

    order = [(dx, dy, dc) for dx in range(4) for dy in range(4) for dc in range(2)][1:]
    for dx, dy, dc in sorted(order, key=lambda t: -(t[0] & 1) - (t[1] & 1) - 2 * (t[0] == 2) - 2 * (t[1] == 2)):
        a2a(panel(dx, dy, 1 - c if dc else c)).start()

    inbuf[sixteen(me), :] = sendbuf[sixteen(me), :]

    def oz_ref(at, core, part):
        rows = pl.ds(pl.multiple_of(lax.rem(at + NZ, NZ) * OZ, 16), OZ)
        return obuf.at[core, pl.ds(part * (16 // PARTS), 16 // PARTS), rows, :]

    def oz(way, step, part, sending):
        hops = step - 1 if sending else step
        ref = oz_ref(z - hops if way == 0 else z + hops, c, part)
        index = (way * UP + step - 1) * PARTS + part
        return remote(ref, ref, oz_s.at[index], oz_r.at[index], dp=up if way == 0 else down)

    def o_side(back, part, core):
        ref = oz_ref(z - back, core, part)
        index = back * PARTS + part
        return remote(ref, ref, os_s.at[index], os_r.at[index], fsdp=sibling)

    def oz_next(step, part):
        if step <= UP:
            oz(0, step, part, False).wait_recv()
            if step < UP:
                oz(0, step + 1, part, True).start()
            o_side(step, part, c).start()
        oz(1, step, part, False).wait_recv()
        if step < DOWN:
            oz(1, step + 1, part, True).start()
        o_side(NZ - step, part, c).start()

    events = iter([(step, part) for step in range(1, DOWN + 1) for part in range(PARTS)])

    def oz_events(count):
        for _ in range(count):
            event = next(events, None)
            if event:
                oz_next(*event)

    @pl.loop(1, 16)
    def _(k):
        ow_from(lax.rem(place + 16 - k, 16)).wait_recv()

    own_out.wait()
    for part in range(PARTS):
        oz(0, 1, part, True).start()
        oz(1, 1, part, True).start()
    for part in range(PARTS):
        o_side(0, part, c).start()

    tokens_in.wait()

    @pl.loop(0, ROWS // 16)
    def _(i):
        rows = pl.ds(pl.multiple_of(i * 16, 16), 16)
        values = tok[rows, :].astype(F32)
        square_mean = jnp.mean(values * values, axis=-1, keepdims=True)
        tok[rows, :] = (values * lax.rsqrt(square_mean + epsilon) * gain[...]).astype(BF16)

    query = z * ROWS + iota((ROWS, 1), 0)
    begin = jnp.zeros((ROWS, 1), I32)
    end = jnp.int32(0)
    for d in range(8):
        end = end + docs[0, d]
        begin = jnp.where(query >= end, end, begin)
    for back in range(BACK + 1):
        key = (z - back) * ROWS + iota((ROWS, ROWS), 1)
        bias[:, pl.ds(back * ROWS, ROWS)] = jnp.where((key <= query) & (key >= begin), 0.0, masked_score)

    ours = peer[...] == me
    arrival = dot(hot(ours), before)
    holder = iota((NF, NF * 2), 0) == (iota((NF, NF * 2), 1) >> 1)
    odd = (iota((NF, NF * 2), 1) & 1) == 1
    slots = []
    for r in range(6):
        found = ours & (arrival == float(r))
        slots.append(jnp.sum(jnp.where(found, slot[...] + 1, 0), axis=1, keepdims=True) - 1)
    selects = []
    for g in range(3):
        places = jnp.sum(jnp.where(holder, jnp.where(odd, slots[2 * g + 1], slots[2 * g]), 0), axis=0, keepdims=True)
        selects.append(hot(iota((96, NF * 2), 0) == places))

    @pl.loop(1, NF)
    def _(k):
        a2a_from(lax.rem(me + NF - k, NF)).wait_recv()

    def panel_rows(f):
        return pl.ds(pl.multiple_of(f * ROWS, ROWS), ROWS)

    for t in range(6):
        spread[t] = inbuf[:, pl.ds(t * LANES, LANES)].astype(F32)
    for part in range(8):
        for h in range(2):
            total = jnp.zeros((96, LANES), F32)
            for g in range(3):
                piece = spread[g * 2 + h, pl.ds(part, NF * 2, stride=8), :].astype(BF16)
                total += dot(selects[g], piece)
            nm[:, pl.ds((part * 2 + h) * LANES, LANES)] = total
            blocks[part * 2 + h] = total
    for k in range(3):
        for part in range(8):
            row, third = divmod(8 * k + part, 3)
            for h in range(2):
                piece = blocks[part * 2 + h, pl.ds(k, 32, stride=3), :]
                spread[third * 2 + h, pl.ds(row, 32, stride=8), :] = piece
    for t in range(6):
        wbuf[panel_rows(me), pl.ds(t * LANES, LANES)] = spread[t, pl.ds(0, ROWS), :].astype(BF16)

    def coords(half, first, second):
        return (first, second) if half == 0 else (second, first)

    def neighbour(axis, step):
        if axis == 0:
            return lax.rem(x + 4 + step, 4) * 8 + y * 2 + c
        return x * 8 + lax.rem(y + 4 + step, 4) * 2 + c

    def ring(stage, half, phase, kind, sending):
        step = 1 if kind in (0, 2) else -1
        arrives = {0: 1, 1: 3, 2: 2, 3: 2}[kind]
        leaves = {0: 0, 1: 0, 2: 1, 3: 3}[kind]
        along = leaves if sending else arrives
        if phase == 0:
            dx, dy = coords(half, along, 0)
            axis = half
        else:
            dx, dy = coords(half, phase - 1, along)
            axis = 1 - half
        start = panel(dx, dy, c) * ROWS + half * 128 + (64 if kind == 3 else 0)
        size = 64 if kind >= 2 else 128
        first, width = COLS[stage]
        ref = wbuf.at[pl.ds(pl.multiple_of(start, 64), size), pl.ds(first, width)]
        index = ((stage * 2 + half) * 5 + phase) * 4 + kind
        return remote(ref, ref, w_s.at[index], w_r.at[index], fsdp=neighbour(axis, step))

    def go(stage, phase, kinds):
        for kind in kinds:
            for half in range(2):
                ring(stage, half, phase, kind, True).start()

    def come(stage, phase, kinds):
        for kind in kinds:
            for half in range(2):
                ring(stage, half, phase, kind, False).wait_recv()

    def side(stage, dx, dy, core):
        first, width = COLS[stage]
        ref = wbuf.at[panel_rows(panel(dx, dy, core)), pl.ds(first, width)]
        index = stage * 16 + dx * 4 + dy
        return remote(ref, ref, sib_s.at[index], sib_r.at[index], fsdp=sibling)

    def share(stage, places):
        for dx, dy in places:
            side(stage, dx, dy, c).start()

    def multiply(stage, places, other):
        first, width = COLS[stage]
        columns = pl.ds(first, width)
        if other:
            for dx, dy in places:
                side(stage, dx, dy, 1 - c).wait_recv()
        rows = [panel_rows(panel(dx, dy, 1 - c if other else c)) for dx, dy in places]
        left = jnp.concatenate([tok[:, r] for r in rows], axis=1)
        right = jnp.concatenate([wbuf[r, columns] for r in rows], axis=0)
        acc[:, columns] += dot(left, right)

    near = [(0, 0)]
    cross = [(1, 0), (3, 0), (0, 1), (0, 3)]
    corner = [(1, 1), (1, 3), (3, 1), (3, 3)]
    two = [(2, 0), (0, 2)]
    knight = [(1, 2), (3, 2), (2, 1), (2, 3)]
    far = [(2, 2)]

    def open_stage(stage):
        go(stage, 0, (0, 1))
        go(stage, 1, (0, 1))
        share(stage, near)

    def step_one(stage):
        come(stage, 0, (0,))
        go(stage, 0, (2,))
        go(stage, 2, (0, 1))
        come(stage, 0, (1,))
        go(stage, 0, (3,))
        go(stage, 4, (0, 1))

    def step_two(stage):
        come(stage, 1, (0,))
        go(stage, 1, (2,))
        come(stage, 1, (1,))
        go(stage, 1, (3,))
        share(stage, cross)

    def step_three(stage):
        come(stage, 0, (2, 3))
        go(stage, 3, (0, 1))

    def step_four(stage):
        for phase in (2, 4):
            come(stage, phase, (0,))
            go(stage, phase, (2,))
            come(stage, phase, (1,))
            go(stage, phase, (3,))
        share(stage, corner)

    def step_five(stage):
        come(stage, 1, (2, 3))
        share(stage, two)
        come(stage, 3, (0,))
        go(stage, 3, (2,))
        come(stage, 3, (1,))
        go(stage, 3, (3,))

    def step_six(stage):
        come(stage, 2, (2, 3))
        come(stage, 4, (2, 3))
        share(stage, knight)

    def step_seven(stage):
        come(stage, 3, (2, 3))
        share(stage, far)

    def kv(step):
        src = kvbuf.at[pl.ds((step - 1) * ROWS, ROWS), :]
        dst = kvbuf.at[pl.ds(step * ROWS, ROWS), :]
        return remote(src, dst, kv_s.at[step - 1], kv_r.at[step - 1], dp=up)

    def kv_send(step):
        @pl.when((z < NZ - 1) & (z >= step - 1))
        def _():
            kv(step).start()

    def kv_sent(step):
        @pl.when((z < NZ - 1) & (z >= step - 1))
        def _():
            kv(step).wait_send()

    def kv_next(step):
        @pl.when(z >= step)
        def _():
            kv(step).wait_recv()

        if step < BACK:
            kv_send(step + 1)

    open_stage(0)
    acc[...] = jnp.zeros_like(acc)
    oz_events(2)
    step_one(0)
    oz_events(1)
    step_two(0)
    oz_events(1)
    multiply(0, near, False)
    open_stage(1)
    step_three(0)
    multiply(0, near, True)
    step_four(0)
    oz_events(1)
    multiply(0, cross, False)
    oz_events(1)
    step_five(0)
    multiply(0, cross, True)
    multiply(0, corner, False)
    oz_events(1)
    step_one(1)
    step_six(0)
    multiply(0, corner + two, True)
    multiply(0, two + knight, False)
    oz_events(1)
    step_two(1)
    step_seven(0)
    multiply(0, knight, True)
    multiply(0, far, False)
    oz_events(1)
    multiply(0, far, True)

    cz, sz = cos_z[pl.ds(z, 1), :], sin_z[pl.ds(z, 1), :]
    cosine = cos_r[...] * cz - sin_r[...] * sz
    sine = sin_r[...] * cz + cos_r[...] * sz
    sine = jnp.where(iota((ROWS, HD), 1) < HD // 2, -sine, sine)

    def rotate(values):
        return (values * cosine + pltpu.roll(values, HD // 2, 1) * sine).astype(BF16)

    kvbuf[pl.ds(0, ROWS), pl.ds(0, HD)] = rotate(acc[:, pl.ds(QW, HD)])
    kvbuf[pl.ds(0, ROWS), pl.ds(HD, HD)] = acc[:, pl.ds(QW + HD, HD)].astype(BF16)
    kv_send(1)
    step_three(1)
    multiply(1, near + cross, False)
    oz_events(1)
    step_four(1)
    kv_next(1)
    multiply(1, near + cross, True)
    oz_events(1)
    multiply(1, corner, False)
    step_five(1)
    kv_next(2)
    oz_events(1)
    multiply(1, corner, True)
    multiply(1, two, False)
    oz_events(1)
    step_six(1)
    kv_next(3)
    multiply(1, knight, False)
    multiply(1, two, True)
    oz_events(1)
    step_seven(1)
    multiply(1, knight, True)
    oz_events(1)
    multiply(1, far, False)
    multiply(1, far, True)
    kv_next(4)

    scale = np.float32(np.log2(np.e) / np.sqrt(HD))
    for h in range(HQ):
        columns = pl.ds(h * HD, HD)
        queries = rotate(acc[:, columns])
        scores = lax.dot_general(
            queries, kvbuf[:, pl.ds(0, HD)], (((1,), (1,)), ((), ())), preferred_element_type=F32
        )
        scores = scores * scale + bias[...]
        expterm = jnp.exp2(scores - jnp.max(scores, axis=1, keepdims=True))
        denom = jnp.sum(expterm, axis=1, keepdims=True)
        att[:, columns] = (dot(expterm.astype(BF16), kvbuf[:, pl.ds(HD, HD)]) / denom).astype(BF16)
        oz_events(1)

    for event in events:
        oz_next(*event)
    for part in range(PARTS):
        for back in range(NZ):
            o_side(back, part, 1 - c).wait_recv()

    @pl.loop(1, NF)
    def _(k):
        a2a(lax.rem(me + k, NF)).wait_send()

    @pl.loop(1, 16)
    def _(k):
        ow_to(k).wait_send()

    for stage in range(2):
        for phase in range(5):
            for kind in range(4):
                for half in range(2):
                    ring(stage, half, phase, kind, True).wait_send()
        for dx in range(4):
            for dy in range(4):
                side(stage, dx, dy, c).wait_send()
    for part in range(PARTS):
        for step in range(1, UP + 1):
            oz(0, step, part, True).wait_send()
        for step in range(1, DOWN + 1):
            oz(1, step, part, True).wait_send()
        for back in range(NZ):
            o_side(back, part, c).wait_send()
    for step in range(1, BACK + 1):
        kv_sent(step)


def project(att, weight, nm_in, out, nm, staged, sem):
    routed = pltpu.make_async_copy(nm_in, nm, sem.at[8])
    routed.start()
    copies = [routed]
    for part in range(8):
        for f in range(part * 4, part * 4 + 4):
            staged[:, pl.ds(f * 256, 256)] = dot(att[...], weight[f % 2, f // 2]).astype(BF16)
        columns = pl.ds(part * 1024, 1024)
        copies.append(pltpu.make_async_copy(staged.at[:, columns], out.at[:, columns], sem.at[part]))
        copies[-1].start()
    for copy in copies:
        copy.wait()


def rotation_tables():
    inverse = theta_base ** (-2.0 * np.arange(HD // 2, dtype=np.float64) / HD)
    inverse = np.concatenate([inverse, inverse])[None, :]
    low = np.arange(ROWS, dtype=np.float64)[:, None] * inverse
    high = np.arange(NZ, dtype=np.float64)[:, None] * ROWS * inverse
    return [t.astype(np.float32) for t in (np.cos(low), np.sin(low), np.cos(high), np.sin(high))]


def per_device(tokens, norm_gain, old_master, route_peer, route_slot, out_weight, doc_lengths):
    vmem = pl.BlockSpec(memory_space=pltpu.VMEM)
    hbm = pl.BlockSpec(memory_space=pl.ANY)
    dma = pltpu.SemaphoreType.DMA
    attended, gathered, routed = pl.pallas_call(
        kernel,
        out_shape=(
            pltpu.VMEM((ROWS, QW), BF16),
            pltpu.VMEM((2, 16, 512, 256), BF16),
            pltpu.VMEM((96, BLK), F32),
        ),
        in_specs=[hbm, vmem, vmem, vmem, vmem, hbm, pl.BlockSpec(memory_space=pltpu.SMEM)] + [vmem] * 4,
        out_specs=(vmem, vmem, vmem),
        scratch_shapes=[
            pltpu.VMEM((ROWS, D), BF16),
            pltpu.VMEM((NF, LANES), I32),
            pltpu.VMEM((NF, LANES), I32),
            pltpu.VMEM((8 * LANES, 256), BF16),
            pltpu.VMEM((6, NF * 16, LANES), F32),
            pltpu.VMEM((16, 96, LANES), F32),
            pltpu.VMEM((NF * 16, W), BF16),
            pltpu.VMEM((NF * 16, W), BF16),
            pltpu.VMEM((D, W), BF16),
            pltpu.VMEM(((BACK + 1) * ROWS, 256), BF16),
            pltpu.VMEM((ROWS, W), F32),
            pltpu.VMEM((ROWS, (BACK + 1) * ROWS), F32),
            dma((3,)),
            dma((NF,)), dma((NF,)),
            dma((80,)), dma((80,)),
            dma((32,)), dma((32,)),
            dma((16,)), dma((16,)),
            dma(((UP + DOWN) * PARTS,)), dma(((UP + DOWN) * PARTS,)),
            dma((NZ * PARTS,)), dma((NZ * PARTS,)),
            dma((4,)), dma((4,)),
        ],
        compiler_params=pltpu.CompilerParams(
            collective_id=0, has_side_effects=True, vmem_limit_bytes=50 * 1024 * 1024
        ),
        cost_estimate=pl.CostEstimate(flops=8 * 10**9, bytes_accessed=10**7, transcendentals=1310720),
    )(
        tokens[0],
        norm_gain[None, :],
        old_master,
        route_peer,
        route_slot,
        out_weight,
        doc_lengths,
        *rotation_tables(),
    )
    update, new_master = pl.pallas_call(
        project,
        out_shape=(jax.ShapeDtypeStruct((ROWS, D), BF16), jax.ShapeDtypeStruct((96, BLK), F32)),
        in_specs=[vmem, vmem, vmem],
        out_specs=(hbm, hbm),
        scratch_shapes=[pltpu.VMEM((ROWS, D), BF16), dma((9,))],
        compiler_params=pltpu.CompilerParams(vmem_limit_bytes=16 * 1024 * 1024),
        cost_estimate=pl.CostEstimate(flops=2 * ROWS * QW * D, bytes_accessed=5 * 10**6, transcendentals=0),
    )(attended, gathered, routed)
    return (update[None], new_master)


def solution(mesh):
    placed = (
        P("fsdp", "dp", None),
        P(),
        P("fsdp", None),
        P(),
        P(),
        P(None, "fsdp"),
        P("fsdp", None),
    )
    return jax.shard_map(
        per_device,
        mesh=mesh,
        in_specs=placed,
        out_specs=(P("fsdp", "dp", None), P("fsdp", None)),
        check_vma=False,
    )
```
